32 devices in a mesh: grp: 2 (over y), row: 16 (over z, x, core).
Axes of the slice: x: 2, y: 2, z: 4, core: 2. Of those that a mesh axis runs over, the one named last changes fastest.
Arguments:
- voltages: bfloat16 [256, 262144], P('grp', 'row'), parts along dimension 0, may hold values from -8 to 8
- taps: float32 [3, 8192], replicated, may hold values from -3 to 3
- station_order: int32 [128], P('grp'), parts along dimension 0, may hold values from 0 to 63, each once
- pair_list: int32 [16, 2], P('grp'), parts along dimension 0, may hold values from 0 to 3, as said below
Outputs:
- visibilities: float32 [2, 4096, 16, 1024], P(None, 'row', 'grp'), parts along dimension 2
The draws below stay inside these ranges and needn't reach their ends.
There are 2 independent parts, one for each index of `grp`. The reference program is written for one: setup_inputs(seed, part) draws one part's arguments, and reference() takes and returns one part's arrays. A program takes and returns all parts, laid end to end along the dimension named above; an argument that names none is the same for every part. Nothing has to cross between parts.
Inputs may be any that keep to these rules, and one draw needn't show every extreme that they name: `station_order`: a permutation of the stations. `pair_list`: distinct pairs (first, second) of block numbers with first <= second, sorted by first and then second; the pair (0, 3) is always listed.
All inputs are finite; a program needn't handle non-finite values.
Results may differ from the reference program's by a relative error of at most 0.0022.
Values may be sent and summed in bfloat16 or wider, within the bound.
A program may use at most 320 MiB of HBM per device.

```python
import math
import jax
import jax.numpy as jnp
import numpy as np
from jax import lax

STATIONS = 64
INPUTS = 128
BLOCK_SIZE = 32
BLOCKS = 4
PAIR_COUNT = 8
TRANSFORM = 8192
CHANNELS = 4096
FILTER_TAPS = 3
SPECTRA = 32
SAMPLES = 262144


def draw_voltages(key, part):
    key = jax.random.fold_in(key, 11)
    key_gain, key_sky, key_noise = jax.random.split(key, 3)
    sky = jax.random.normal(key_sky, (1, SAMPLES), jnp.float32)
    gains = jax.random.uniform(key_gain, (INPUTS, 1), jnp.float32, 0.3, 0.9)
    noise = jax.random.normal(key_noise, (INPUTS, SAMPLES), jnp.float32)
    return jnp.clip(gains * sky + noise, -8.0, 8.0).astype(jnp.bfloat16)


def draw_pair_list(key, part):
    key = jax.random.fold_in(key, 5)
    triangle = BLOCKS * (BLOCKS + 1) // 2
    others = jax.random.permutation(key, triangle - 1)[:PAIR_COUNT - 1].astype(jnp.int32)
    others = others + (others >= BLOCKS - 1).astype(jnp.int32)
    chosen = jnp.sort(jnp.concatenate([jnp.full((1,), BLOCKS - 1, jnp.int32), others]))
    first_table, second_table = np.triu_indices(BLOCKS)
    first_values = jnp.take(jnp.asarray(first_table, jnp.int32), chosen)
    second_values = jnp.take(jnp.asarray(second_table, jnp.int32), chosen)
    return jnp.stack([first_values, second_values], 1).astype(jnp.int32)


def gaussian(stream_key, dims, width, bound, kind=jnp.bfloat16):
    values = width * jax.random.normal(stream_key, dims, jnp.float32)
    return jnp.clip(values, min=-bound, max=bound).astype(kind)


def setup_inputs(seed: int = 0, part: int = 0) -> dict:
    streams_of = jax.random.split(jax.random.key(seed), 5)
    part_splits = jax.random.split(jax.random.fold_in(streams_of[4], part), 5)
    voltages = draw_voltages(jax.random.fold_in(jax.random.fold_in(streams_of[4], part), 71), part)
    taps = gaussian(streams_of[1], (FILTER_TAPS, TRANSFORM), 0.6, 3.0, jnp.float32)
    station_order = jax.random.permutation(part_splits[2], STATIONS).astype(jnp.int32)
    pair_list = draw_pair_list(jax.random.fold_in(jax.random.fold_in(streams_of[4], part), 71), part)
    return dict(voltages=voltages, taps=taps, station_order=station_order, pair_list=pair_list)


def input_order(station_order):
    station_count = station_order.shape[0]
    position = jnp.arange(2 * station_count, dtype=jnp.int32)
    return (2 * jnp.take(station_order, position // 2) + position % 2).astype(jnp.int32)

def reference(voltages, taps, station_order, pair_list):

    def one_input(series):
        blocks_now = series.astype(jnp.float32).reshape(SPECTRA, TRANSFORM)
        padded = jnp.concatenate([jnp.zeros((FILTER_TAPS - 1, TRANSFORM), jnp.float32), blocks_now], 0)
        filtered = jnp.zeros((SPECTRA, TRANSFORM), jnp.float32)
        for tap_index in range(FILTER_TAPS):
            filtered = filtered + taps[tap_index][None, :] * padded[tap_index:tap_index + SPECTRA]
        spectrum = jnp.fft.rfft(filtered, axis=1)[:, :CHANNELS] * (1.0 / math.sqrt(TRANSFORM))
        return jnp.stack([spectrum.real, spectrum.imag]).astype(jnp.bfloat16)
    spectra_all = lax.map(one_input, voltages)
    order = input_order(station_order)
    grouped = order.reshape(BLOCKS, BLOCK_SIZE)
    left_rows = jnp.take(grouped, pair_list[:, 0], axis=0)
    right_rows = jnp.take(grouped, pair_list[:, 1], axis=0)
    channel_major = jnp.transpose(spectra_all, (3, 1, 2, 0))
    group_size = math.gcd(CHANNELS, 32)
    grouped_channels = channel_major.reshape(CHANNELS // group_size, group_size, 2, SPECTRA, INPUTS)

    def one_group(block_now):
        real_part = block_now[:, 0].astype(jnp.float32)
        imag_part = block_now[:, 1].astype(jnp.float32)

        def select(values, chosen):
            picked = jnp.take(values, chosen.reshape(-1), axis=2)
            return picked.reshape(group_size, SPECTRA, PAIR_COUNT, BLOCK_SIZE)

        def product(operand_one, operand_two):
            return jnp.einsum('cspa,cspb->cpab', operand_one, operand_two)
        left_real = select(real_part, left_rows)
        left_imag = select(imag_part, left_rows)
        right_real = select(real_part, right_rows)
        right_imag = select(imag_part, right_rows)
        vis_real = product(left_real, right_real) + product(left_imag, right_imag)
        vis_imag = product(left_imag, right_real) - product(left_real, right_imag)
        return jnp.stack([vis_real, vis_imag]) * (1.0 / SPECTRA)
    result = lax.map(one_group, grouped_channels)
    result = jnp.transpose(result, (1, 0, 2, 3, 4, 5))
    return result.reshape(2, CHANNELS, PAIR_COUNT, BLOCK_SIZE * BLOCK_SIZE)
```

```python
import functools
import math

import jax
import jax.numpy as jnp
import numpy as np
from jax import lax
from jax.experimental import pallas as pl
from jax.experimental.pallas import tpu as pltpu
from jax.sharding import PartitionSpec as P

BLOCK_SIZE = 32
LANES = 128
RADIX = 64
HALF = RADIX // 2
ROWS = 16
VMEM_BYTES = 56 * 1024 * 1024


def dft_tables(length):
    a = np.arange(LANES)
    k1 = np.arange(HALF + 1)
    angle = 2.0 * np.pi * ((k1[:, None] * a[None, :]) % length) / length
    twist = np.stack([np.cos(angle), np.sin(angle)]).astype(np.float32)
    low = np.arange(RADIX)
    high = LANES - 1 - low

    def rows(k2, sign):
        ang = 2.0 * np.pi * ((k2[:, None] * a[None, :]) % LANES) / LANES
        c, s = np.cos(ang), np.sin(ang)
        real = np.concatenate([c, s], 1)
        imag = np.concatenate([-s, c], 1) * sign
        return [real, imag]

    table = np.concatenate(rows(low, 1.0) + rows(high, -1.0), 0) / math.sqrt(length)
    table_hi = table.astype(np.float32).astype(jnp.bfloat16)
    table_lo = (table - table_hi.astype(np.float64)).astype(np.float32).astype(jnp.bfloat16)
    return twist, np.stack([table_hi, table_lo])


def add(x, y):
    return (x[0] + y[0], none_add(x[1], y[1]))


def none_add(x, y):
    if x is None:
        return y
    return x if y is None else x + y


def none_sub(x, y):
    if y is None:
        return x
    return -y if x is None else x - y


def sub(x, y):
    return (x[0] - y[0], none_sub(x[1], y[1]))


def times(x, c, s):
    re, im = x
    if abs(s) < 1e-12:
        return x if c > 0 else (-re, None if im is None else -im)
    if abs(c) < 1e-12:
        if s > 0:
            return (jnp.zeros_like(re) if im is None else im, -re)
        return (jnp.zeros_like(re) if im is None else -im, re)
    if im is None:
        return (re * c, re * (-s))
    if abs(abs(c) - abs(s)) < 1e-12:
        r = abs(c)
        sc, ss = (1 if c > 0 else -1), (1 if s > 0 else -1)
        p = re + im if sc == ss else re - im
        q = im - re if sc == ss else im + re
        return (p * (r * sc), q * (r * sc))
    return (re * c + im * s, im * c - re * s)


def fft_list(xs):
    n = len(xs)
    if n == 1:
        return xs
    even, odd = fft_list(xs[0::2]), fft_list(xs[1::2])
    out = [None] * n
    for k in range(n // 2):
        ang = 2.0 * math.pi * k / n
        t = times(odd[k], math.cos(ang), math.sin(ang))
        out[k] = add(even[k], t)
        out[k + n // 2] = sub(even[k], t)
    return out


def real_dft64(xs):
    first = [fft_list([(xs[8 * b1 + b0], None) for b1 in range(8)]) for b0 in range(8)]
    out = {}
    for k in range(5):
        terms = []
        for b0 in range(8):
            ang = 2.0 * math.pi * b0 * k / 64
            terms.append(times(first[b0][k], math.cos(ang), math.sin(ang)))
        res = fft_list(terms)
        for j in range(8):
            k1 = k + 8 * j
            if k1 <= 32:
                out[k1] = res[j]
            elif 64 - k1 not in out:
                re, im = res[j]
                out[64 - k1] = (re, None if im is None else -im)
    return out


def fft_kernel(now_ref, past_ref, taps_ref, twist_ref, table_ref, out_ref, z_hi, z_lo, spec):
    inputs = now_ref.shape[0]
    spectra = now_ref.shape[1] // (RADIX * LANES)
    length = RADIX * LANES
    group = out_ref.shape[3]
    groups = out_ref.shape[0]

    for s in range(spectra):

        @pl.loop(0, inputs // ROWS)
        def _(step):
            r0 = pl.multiple_of(step * ROWS, ROWS)
            xs = []
            for b in range(RADIX):
                lanes = b * LANES
                total = None
                for t in range(3):
                    block = s + t - 2
                    if block < 0:
                        ref, off = past_ref, (block + 2) * length + lanes
                    else:
                        ref, off = now_ref, block * length + lanes
                    term = taps_ref[t : t + 1, lanes : lanes + LANES] * ref[
                        pl.ds(r0, ROWS), off : off + LANES
                    ].astype(jnp.float32)
                    total = term if total is None else total + term
                xs.append(total)
            values = real_dft64(xs)
            for k1 in range(HALF + 1):
                re, im = values[k1]
                if k1 == 0:
                    parts = (re, jnp.zeros_like(re))
                else:
                    c = twist_ref[0, k1 : k1 + 1, :]
                    n = twist_ref[1, k1 : k1 + 1, :]
                    if im is None:
                        parts = (re * c, -(re * n))
                    else:
                        parts = (re * c + im * n, im * c - re * n)
                for i, part in enumerate(parts):
                    hi = part.astype(jnp.bfloat16)
                    lo = (part - hi.astype(jnp.float32)).astype(jnp.bfloat16)
                    z_hi[k1, pl.ds(r0, ROWS), i * LANES : (i + 1) * LANES] = hi
                    z_lo[k1, pl.ds(r0, ROWS), i * LANES : (i + 1) * LANES] = lo

        def second(k1, rows):
            dims = (((1,), (1,)), ((), ()))
            hi, lo = z_hi[k1], z_lo[k1]
            w_hi, w_lo = table_ref[0, :rows, :], table_ref[1, :rows, :]
            dot = functools.partial(
                lax.dot_general, dimension_numbers=dims, preferred_element_type=jnp.float32
            )
            o = dot(w_hi, hi) + dot(w_hi, lo) + dot(w_lo, hi)
            for c in range(2):
                spec[c, pl.ds(k1, RADIX, stride=RADIX), :] = o[c * RADIX : (c + 1) * RADIX]
                if rows > 2 * RADIX:
                    spec[c, pl.ds(RADIX - k1, RADIX, stride=RADIX), :] = o[
                        (2 + c) * RADIX : (3 + c) * RADIX
                    ]

        second(0, 2 * RADIX)
        second(HALF, 2 * RADIX)

        @pl.loop(1, HALF)
        def _(k1):
            second(k1, 4 * RADIX)

        @pl.loop(0, groups)
        def _(g):
            for c in range(2):
                out_ref[g, s, c] = spec[c, pl.ds(pl.multiple_of(g * group, group), group), :].astype(
                    jnp.bfloat16
                )


def spectra_of(now, past, taps, groups):
    inputs, samples = now.shape
    length = taps.shape[1]
    assert length == RADIX * LANES and inputs == LANES and taps.shape[0] == 3
    spectra = samples // length
    assert spectra == 2
    channels = length // 2
    twist, table = dft_tables(length)
    vmem = pl.BlockSpec(memory_space=pltpu.VMEM)
    return pl.pallas_call(
        fft_kernel,
        out_shape=jax.ShapeDtypeStruct(
            (groups, spectra, 2, channels // groups, inputs), jnp.bfloat16
        ),
        in_specs=[vmem] * 5,
        out_specs=vmem,
        scratch_shapes=[
            pltpu.VMEM((HALF + 1, inputs, 2 * LANES), jnp.bfloat16),
            pltpu.VMEM((HALF + 1, inputs, 2 * LANES), jnp.bfloat16),
            pltpu.VMEM((2, channels, inputs), jnp.float32),
        ],
        compiler_params=pltpu.CompilerParams(vmem_limit_bytes=VMEM_BYTES),
        cost_estimate=pl.CostEstimate(
            flops=10_000_000_000, bytes_accessed=12_000_000, transcendentals=0
        ),
    )(now, past, taps, jnp.asarray(twist), jnp.asarray(table))


def pair_kernel(scale, pair_ref, data_ref, pick_ref, out_ref, turned, gram, rows_ref):
    depth, chunk, inputs = data_ref.shape
    pairs = out_ref.shape[2]
    half = depth // 2
    data = data_ref[...].reshape(depth * chunk, inputs)
    turned[...] = jnp.dot(data, pick_ref[...], preferred_element_type=jnp.float32)
    lane_group = lax.broadcasted_iota(jnp.int32, (8, LANES), 1) // BLOCK_SIZE

    @pl.loop(0, chunk)
    def _(ch):
        re = turned[pl.ds(ch, half, stride=2 * chunk), :]
        im = turned[pl.ds(chunk + ch, half, stride=2 * chunk), :]
        left = jnp.concatenate([re, im], 0).astype(jnp.bfloat16)
        swapped = jnp.concatenate([-im, re], 0).astype(jnp.bfloat16)
        dims = (((0,), (0,)), ((), ()))
        for c, right in enumerate((left, swapped)):
            gram[c] = lax.dot_general(left, right, dims, preferred_element_type=jnp.float32)
        for c in range(2):
            for p in range(pairs):
                first, second = pair_ref[p, 0], pair_ref[p, 1]
                tile = None
                for j in range(4):
                    piece = gram[c, pl.ds(first * BLOCK_SIZE + j, 8, stride=4), :]
                    amount = lax.rem(j - second + 4, 4) * BLOCK_SIZE
                    piece = pltpu.roll(piece, amount, 1)
                    tile = piece if tile is None else jnp.where(lane_group == j, piece, tile)
                rows_ref[c, pl.ds(p, 8, stride=pairs), :] = tile
            for t in range(8):
                out_ref[c, ch, :, t * LANES : (t + 1) * LANES] = (
                    rows_ref[c, t * pairs : (t + 1) * pairs, :] * scale
                )


def visibilities_of(gathered, pick, pair_list, scale):
    depth, channels, inputs = gathered.shape
    pairs = pair_list.shape[0]
    chunk = min(32, channels)
    return pl.pallas_call(
        functools.partial(pair_kernel, scale),
        grid_spec=pltpu.PrefetchScalarGridSpec(
            num_scalar_prefetch=1,
            grid=(channels // chunk,),
            in_specs=[
                pl.BlockSpec((depth, chunk, inputs), lambda i, _: (0, i, 0)),
                pl.BlockSpec((inputs, inputs), lambda i, _: (0, 0)),
            ],
            out_specs=pl.BlockSpec(
                (2, chunk, pairs, BLOCK_SIZE * BLOCK_SIZE), lambda i, _: (0, i, 0, 0)
            ),
            scratch_shapes=[
                pltpu.VMEM((depth * chunk, inputs), jnp.float32),
                pltpu.VMEM((2, inputs, inputs), jnp.float32),
                pltpu.VMEM((2, 8 * pairs, LANES), jnp.float32),
            ],
        ),
        out_shape=jax.ShapeDtypeStruct(
            (2, channels, pairs, BLOCK_SIZE * BLOCK_SIZE), jnp.float32
        ),
        compiler_params=pltpu.CompilerParams(
            vmem_limit_bytes=VMEM_BYTES, dimension_semantics=("arbitrary",)
        ),
        cost_estimate=pl.CostEstimate(
            flops=4_000_000_000, bytes_accessed=20_000_000, transcendentals=0
        ),
    )(pair_list, gathered, pick)


def input_order(station_order):
    return (2 * station_order[:, None] + jnp.arange(2, dtype=jnp.int32)[None, :]).reshape(-1)


def shards(row_count, voltages, taps, station_order, pair_list):
    order = input_order(station_order)
    inputs = voltages.shape[0]
    pick = (jnp.arange(inputs, dtype=jnp.int32)[:, None] == order[None, :]).astype(jnp.bfloat16)
    past = lax.ppermute(voltages, "row", [(i, i + 1) for i in range(row_count - 1)])
    spectra = spectra_of(voltages, past, taps, row_count)
    gathered = lax.all_to_all(spectra, "row", split_axis=0, concat_axis=0, tiled=True)
    spectra_total = row_count * spectra.shape[1]
    gathered = gathered.reshape(spectra_total * 2, spectra.shape[3], inputs)
    return visibilities_of(gathered, pick, pair_list, 1.0 / spectra_total)


def solution(mesh):
    placed = (P("grp", "row"), P(), P("grp"), P("grp", None))
    return jax.shard_map(
        functools.partial(shards, mesh.shape["row"]),
        mesh=mesh,
        in_specs=placed,
        out_specs=P(None, "row", "grp", None),
        check_vma=False,
    )
```

```python
import functools
import math

import jax
import jax.numpy as jnp
import numpy as np
from jax import lax
from jax.experimental import pallas as pl
from jax.experimental.pallas import tpu as pltpu
from jax.sharding import PartitionSpec as P

BLOCK_SIZE = 32
LANES = 128
RADIX = 64
HALF = RADIX // 2
ROWS = 16
UNROLL = 16
PIECES = 2
VMEM_BYTES = 56 * 1024 * 1024


def dft_tables(length):
    a = np.arange(LANES)
    k1 = np.arange(HALF + 1)
    angle = 2.0 * np.pi * ((k1[:, None] * a[None, :]) % length) / length
    twist = np.stack([np.cos(angle), np.sin(angle)]).astype(np.float32)
    low = np.arange(RADIX)
    high = LANES - 1 - low

    def rows(k2, sign):
        ang = 2.0 * np.pi * ((k2[:, None] * a[None, :]) % LANES) / LANES
        c, s = np.cos(ang), np.sin(ang)
        real = np.concatenate([c, s], 1)
        imag = np.concatenate([-s, c], 1) * sign
        return [real, imag]

    table = np.concatenate(rows(low, 1.0) + rows(high, -1.0), 0) / math.sqrt(length)
    table_hi = table.astype(np.float32).astype(jnp.bfloat16)
    table_lo = (table - table_hi.astype(np.float64)).astype(np.float32).astype(jnp.bfloat16)
    return twist, np.stack([table_hi, table_lo])


def add(x, y):
    return (x[0] + y[0], none_add(x[1], y[1]))


def none_add(x, y):
    if x is None:
        return y
    return x if y is None else x + y


def none_sub(x, y):
    if y is None:
        return x
    return -y if x is None else x - y


def sub(x, y):
    return (x[0] - y[0], none_sub(x[1], y[1]))


def times(x, c, s):
    re, im = x
    if abs(s) < 1e-12:
        return x if c > 0 else (-re, None if im is None else -im)
    if abs(c) < 1e-12:
        if s > 0:
            return (jnp.zeros_like(re) if im is None else im, -re)
        return (jnp.zeros_like(re) if im is None else -im, re)
    if im is None:
        return (re * c, re * (-s))
    if abs(abs(c) - abs(s)) < 1e-12:
        r = abs(c)
        sc, ss = (1 if c > 0 else -1), (1 if s > 0 else -1)
        p = re + im if sc == ss else re - im
        q = im - re if sc == ss else im + re
        return (p * (r * sc), q * (r * sc))
    return (re * c + im * s, im * c - re * s)


def fft_list(xs):
    n = len(xs)
    if n == 1:
        return xs
    even, odd = fft_list(xs[0::2]), fft_list(xs[1::2])
    out = [None] * n
    for k in range(n // 2):
        ang = 2.0 * math.pi * k / n
        t = times(odd[k], math.cos(ang), math.sin(ang))
        out[k] = add(even[k], t)
        out[k + n // 2] = sub(even[k], t)
    return out


def real_dft64(xs):
    first = [fft_list([(xs[8 * b1 + b0], None) for b1 in range(8)]) for b0 in range(8)]
    out = {}
    for k in range(5):
        terms = []
        for b0 in range(8):
            ang = 2.0 * math.pi * b0 * k / 64
            terms.append(times(first[b0][k], math.cos(ang), math.sin(ang)))
        res = fft_list(terms)
        for j in range(8):
            k1 = k + 8 * j
            if k1 <= 32:
                out[k1] = res[j]
            elif 64 - k1 not in out:
                re, im = res[j]
                out[64 - k1] = (re, None if im is None else -im)
    return out


def fft_kernel(old_ref, mid_ref, new_ref, taps_ref, twist_ref, table_ref, *rest):
    *out_refs, z_hi, z_lo, spec = rest
    inputs = new_ref.shape[0]
    groups = out_refs[0].shape[0]
    group = sum(ref.shape[2] for ref in out_refs)

    @pl.loop(0, inputs // ROWS)
    def _(step):
        r0 = pl.multiple_of(step * ROWS, ROWS)
        xs = []
        for b in range(RADIX):
            lanes = slice(b * LANES, (b + 1) * LANES)
            total = None
            for t, ref in enumerate((old_ref, mid_ref, new_ref)):
                term = taps_ref[t : t + 1, lanes] * ref[pl.ds(r0, ROWS), lanes].astype(jnp.float32)
                total = term if total is None else total + term
            xs.append(total)
        values = real_dft64(xs)
        for k1 in range(HALF + 1):
            re, im = values[k1]
            if k1 == 0:
                parts = (re, jnp.zeros_like(re))
            else:
                c = twist_ref[0, k1 : k1 + 1, :]
                n = twist_ref[1, k1 : k1 + 1, :]
                if im is None:
                    parts = (re * c, -(re * n))
                else:
                    parts = (re * c + im * n, im * c - re * n)
            for i, part in enumerate(parts):
                hi = part.astype(jnp.bfloat16)
                lo = (part - hi.astype(jnp.float32)).astype(jnp.bfloat16)
                z_hi[k1, pl.ds(r0, ROWS), i * LANES : (i + 1) * LANES] = hi
                z_lo[k1, pl.ds(r0, ROWS), i * LANES : (i + 1) * LANES] = lo

    def second(k1, rows):
        dims = (((1,), (1,)), ((), ()))
        hi, lo = z_hi[k1], z_lo[k1]
        w_hi, w_lo = table_ref[0, :rows, :], table_ref[1, :rows, :]
        dot = functools.partial(
            lax.dot_general, dimension_numbers=dims, preferred_element_type=jnp.float32
        )
        o = dot(w_hi, hi) + dot(w_hi, lo) + dot(w_lo, hi)
        for c in range(2):
            spec[c, pl.ds(k1, RADIX, stride=RADIX), :] = o[c * RADIX : (c + 1) * RADIX]
            if rows > 2 * RADIX:
                spec[c, pl.ds(RADIX - k1, RADIX, stride=RADIX), :] = o[
                    (2 + c) * RADIX : (3 + c) * RADIX
                ]

    second(0, 2 * RADIX)
    second(HALF, 2 * RADIX)

    @pl.loop(1, HALF)
    def _(k1):
        second(k1, 4 * RADIX)

    @pl.loop(0, groups)
    def _(g):
        for c in range(2):
            start = g * group
            for ref in out_refs:
                size = ref.shape[2]
                ref[g, c] = spec[c, pl.ds(pl.multiple_of(start, size), size), :].astype(jnp.bfloat16)
                start = start + size


def spectrum_of(old, mid, new, taps, groups, pieces):
    inputs = new[0].shape[0]
    length = taps.shape[1]
    assert length == RADIX * LANES and inputs == LANES and taps.shape[0] == 3
    channels = length // 2
    size = channels // groups // pieces
    twist, table = dft_tables(length)

    def block(index):
        return pl.BlockSpec((inputs, length), lambda i: (0, index))

    def whole(array):
        return pl.BlockSpec(array.shape, lambda i: (0,) * array.ndim)

    out = jax.ShapeDtypeStruct((groups, 2, size, inputs), jnp.bfloat16)
    return pl.pallas_call(
        fft_kernel,
        grid=(1,),
        out_shape=[out] * pieces,
        in_specs=[block(old[1]), block(mid[1]), block(new[1]), whole(taps), whole(twist), whole(table)],
        out_specs=[whole(out)] * pieces,
        scratch_shapes=[
            pltpu.VMEM((HALF + 1, inputs, 2 * LANES), jnp.bfloat16),
            pltpu.VMEM((HALF + 1, inputs, 2 * LANES), jnp.bfloat16),
            pltpu.VMEM((2, channels, inputs), jnp.float32),
        ],
        compiler_params=pltpu.CompilerParams(vmem_limit_bytes=VMEM_BYTES),
        cost_estimate=pl.CostEstimate(
            flops=12_000_000_000, bytes_accessed=8_000_000, transcendentals=0
        ),
    )(old[0], mid[0], new[0], taps, jnp.asarray(twist), jnp.asarray(table))


def pair_kernel(scale, pair_ref, late_ref, early_ref, pick_ref, *rest):
    out_ref, turned_left, turned_right, gram = rest[-4:]
    depth, chunk, inputs = late_ref.shape
    rows = depth * chunk
    depth = 2 * depth
    pairs = pair_ref.shape[0]
    half = depth // 2
    for i, ref in enumerate((late_ref, early_ref)):
        data = ref[...].reshape(rows, inputs)
        for side, turned in enumerate((turned_left, turned_right)):
            turned[i * rows : (i + 1) * rows, :] = jnp.dot(
                data, pick_ref[side], preferred_element_type=jnp.float32
            )
    lane_group = lax.broadcasted_iota(jnp.int32, (8, LANES), 1) // BLOCK_SIZE
    masks = [lane_group == j for j in range(4)]
    firsts = [pl.multiple_of(pair_ref[p, 0] * BLOCK_SIZE, BLOCK_SIZE) for p in range(pairs)]
    shifts = [
        [lax.rem(j - pair_ref[p, 1] + 4, 4) * BLOCK_SIZE for j in range(4)] for p in range(pairs)
    ]
    dims = (((0,), (0,)), ((), ()))
    unroll = gram.shape[0]

    @pl.loop(0, chunk // unroll)
    def _(step):
        for i in range(unroll):
            ch = step * unroll + i

            def operand(ref):
                re = ref[pl.ds(ch, half, stride=2 * chunk), :]
                im = ref[pl.ds(chunk + ch, half, stride=2 * chunk), :]
                return re, im

            re, im = operand(turned_left)
            left = jnp.concatenate([re, im], 0).astype(jnp.bfloat16)
            re, im = operand(turned_right)
            re, im = re * scale, im * scale
            right = jnp.concatenate(
                [jnp.concatenate([re, im], 0), jnp.concatenate([-im, re], 0)], 1
            ).astype(jnp.bfloat16)
            gram[i] = lax.dot_general(left, right, dims, preferred_element_type=jnp.float32)
        for i in range(unroll):
            ch = step * unroll + i
            for c in range(2):
                for p in range(pairs):
                    tile = None
                    for j in range(4):
                        piece = gram[
                            i, pl.ds(firsts[p] + 8 * j, 8), c * LANES : (c + 1) * LANES
                        ]
                        piece = pltpu.roll(piece, shifts[p][j], 1)
                        tile = piece if tile is None else jnp.where(masks[j], piece, tile)
                    out_ref[c, ch, pl.ds(p, 8, stride=pairs), :] = tile


def visibilities_of(late, early, base, pick, pair_list, scale, channels, earlier):
    depth, size, inputs = early.shape
    pairs = pair_list.shape[0]
    chunk = min(32, size)
    first = base // chunk
    operands = [pair_list, late, early, pick]
    in_specs = [
        pl.BlockSpec((depth, chunk, inputs), lambda i, _: (0, first + i, 0)),
        pl.BlockSpec((depth, chunk, inputs), lambda i, _: (0, i, 0)),
        pl.BlockSpec((2, inputs, inputs), lambda i, _: (0, 0, 0)),
    ]
    aliases = {}
    if earlier is not None:
        aliases = {len(operands): 0}
        operands.append(earlier)
        in_specs.append(pl.BlockSpec(memory_space=pl.ANY))
    return pl.pallas_call(
        functools.partial(pair_kernel, scale),
        grid_spec=pltpu.PrefetchScalarGridSpec(
            num_scalar_prefetch=1,
            grid=(size // chunk,),
            in_specs=in_specs,
            out_specs=pl.BlockSpec(
                (2, chunk, 8 * pairs, LANES), lambda i, _: (0, first + i, 0, 0)
            ),
            scratch_shapes=[
                pltpu.VMEM((2 * depth * chunk, inputs), jnp.float32),
                pltpu.VMEM((2 * depth * chunk, inputs), jnp.float32),
                pltpu.VMEM((min(UNROLL, chunk), inputs, 2 * inputs), jnp.float32),
            ],
        ),
        out_shape=jax.ShapeDtypeStruct((2, channels, 8 * pairs, LANES), jnp.float32),
        input_output_aliases=aliases,
        compiler_params=pltpu.CompilerParams(
            vmem_limit_bytes=VMEM_BYTES, dimension_semantics=("arbitrary",)
        ),
        cost_estimate=pl.CostEstimate(
            flops=20_000_000_000 // (channels // size), bytes_accessed=20_000_000, transcendentals=0
        ),
    )(*operands)


def input_order(station_order):
    return (2 * station_order[:, None] + jnp.arange(2, dtype=jnp.int32)[None, :]).reshape(-1)


def shards(row_count, voltages, taps, station_order, pair_list):
    order = input_order(station_order)
    inputs = voltages.shape[0]
    left_order = jnp.swapaxes(order.reshape(-1, BLOCK_SIZE // 4, 4), 1, 2).reshape(-1)
    both = jnp.stack([left_order, order])
    pick = (jnp.arange(inputs, dtype=jnp.int32)[None, :, None] == both[:, None, :]).astype(jnp.bfloat16)
    length = taps.shape[1]
    assert voltages.shape[1] == 2 * length
    onward = [(i, i + 1) for i in range(row_count - 1)]
    past_two = lax.ppermute(voltages[:, length:], "row", onward)
    sent, past_two = lax.optimization_barrier((voltages[:, :length], past_two))
    past_one = lax.ppermute(sent, "row", onward)
    channels = length // 2 // row_count

    def exchange(piece):
        moved = lax.all_to_all(piece, "row", split_axis=0, concat_axis=0, tiled=True)
        return moved.reshape(2 * row_count, piece.shape[2], inputs)

    (second,) = spectrum_of((past_two, 0), (voltages, 0), (voltages, 1), taps, row_count, 1)
    late = exchange(second)
    firsts = spectrum_of((past_one, 0), (past_two, 0), (voltages, 0), taps, row_count, PIECES)
    result = None
    for index, piece in enumerate(firsts):
        early = exchange(piece)
        base = index * early.shape[1]
        result = visibilities_of(
            late, early, base, pick, pair_list, 1.0 / (2 * row_count), channels, result
        )
    pairs = pair_list.shape[0]
    tiles = result.reshape(2, channels, 8, pairs, LANES)
    return jnp.swapaxes(tiles, 2, 3).reshape(2, channels, pairs, BLOCK_SIZE * BLOCK_SIZE)


def solution(mesh):
    placed = (P("grp", "row"), P(), P("grp"), P("grp", None))
    return jax.shard_map(
        functools.partial(shards, mesh.shape["row"]),
        mesh=mesh,
        in_specs=placed,
        out_specs=P(None, "row", "grp", None),
        check_vma=False,
    )
```

```python
import functools
import math

import jax
import jax.numpy as jnp
import numpy as np
from jax import lax
from jax.experimental import pallas as pl
from jax.experimental.pallas import tpu as pltpu
from jax.sharding import PartitionSpec as P

BLOCK_SIZE = 32
LANES = 128
RADIX = 64
HALF = RADIX // 2
ROWS = 16
UNROLL = 16
PIECES = 2
VMEM_BYTES = 56 * 1024 * 1024


def dft_tables(length):
    a = np.arange(LANES)
    k1 = np.arange(HALF + 1)
    angle = 2.0 * np.pi * ((k1[:, None] * a[None, :]) % length) / length
    twist = np.stack([np.cos(angle), np.sin(angle)]).astype(np.float32)
    low = np.arange(RADIX)
    high = LANES - 1 - low

    def rows(k2, sign):
        ang = 2.0 * np.pi * ((k2[:, None] * a[None, :]) % LANES) / LANES
        c, s = np.cos(ang), np.sin(ang)
        real = np.concatenate([c, s], 1)
        imag = np.concatenate([-s, c], 1) * sign
        return [real, imag]

    table = np.concatenate(rows(low, 1.0) + rows(high, -1.0), 0) / math.sqrt(length)
    table_hi = table.astype(np.float32).astype(jnp.bfloat16)
    table_lo = (table - table_hi.astype(np.float64)).astype(np.float32).astype(jnp.bfloat16)
    return twist, np.stack([table_hi, table_lo])


def add(x, y):
    return (x[0] + y[0], none_add(x[1], y[1]))


def none_add(x, y):
    if x is None:
        return y
    return x if y is None else x + y


def none_sub(x, y):
    if y is None:
        return x
    return -y if x is None else x - y


def sub(x, y):
    return (x[0] - y[0], none_sub(x[1], y[1]))


def times(x, c, s):
    re, im = x
    if abs(s) < 1e-12:
        return x if c > 0 else (-re, None if im is None else -im)
    if abs(c) < 1e-12:
        if s > 0:
            return (jnp.zeros_like(re) if im is None else im, -re)
        return (jnp.zeros_like(re) if im is None else -im, re)
    if im is None:
        return (re * c, re * (-s))
    if abs(abs(c) - abs(s)) < 1e-12:
        r = abs(c)
        sc, ss = (1 if c > 0 else -1), (1 if s > 0 else -1)
        p = re + im if sc == ss else re - im
        q = im - re if sc == ss else im + re
        return (p * (r * sc), q * (r * sc))
    return (re * c + im * s, im * c - re * s)


def fft_list(xs):
    n = len(xs)
    if n == 1:
        return xs
    even, odd = fft_list(xs[0::2]), fft_list(xs[1::2])
    out = [None] * n
    for k in range(n // 2):
        ang = 2.0 * math.pi * k / n
        t = times(odd[k], math.cos(ang), math.sin(ang))
        out[k] = add(even[k], t)
        out[k + n // 2] = sub(even[k], t)
    return out


def real_dft64(xs):
    first = [fft_list([(xs[8 * b1 + b0], None) for b1 in range(8)]) for b0 in range(8)]
    out = {}
    for k in range(5):
        terms = []
        for b0 in range(8):
            ang = 2.0 * math.pi * b0 * k / 64
            terms.append(times(first[b0][k], math.cos(ang), math.sin(ang)))
        res = fft_list(terms)
        for j in range(8):
            k1 = k + 8 * j
            if k1 <= 32:
                out[k1] = res[j]
            elif 64 - k1 not in out:
                re, im = res[j]
                out[64 - k1] = (re, None if im is None else -im)
    return out


def fft_kernel(old_ref, mid_ref, new_ref, taps_ref, twist_ref, table_ref, *rest):
    *out_refs, z_hi, z_lo, spec = rest
    inputs = new_ref.shape[0]
    groups = out_refs[0].shape[0]
    group = sum(ref.shape[2] for ref in out_refs)

    @pl.loop(0, inputs // ROWS)
    def _(step):
        r0 = pl.multiple_of(step * ROWS, ROWS)
        xs = []
        for b in range(RADIX):
            lanes = slice(b * LANES, (b + 1) * LANES)
            total = None
            for t, ref in enumerate((old_ref, mid_ref, new_ref)):
                term = taps_ref[t : t + 1, lanes] * ref[pl.ds(r0, ROWS), lanes].astype(jnp.float32)
                total = term if total is None else total + term
            xs.append(total)
        values = real_dft64(xs)
        for k1 in range(HALF + 1):
            re, im = values[k1]
            if k1 == 0:
                parts = (re, jnp.zeros_like(re))
            else:
                c = twist_ref[0, k1 : k1 + 1, :]
                n = twist_ref[1, k1 : k1 + 1, :]
                if im is None:
                    parts = (re * c, -(re * n))
                else:
                    parts = (re * c + im * n, im * c - re * n)
            for i, part in enumerate(parts):
                hi = part.astype(jnp.bfloat16)
                lo = (part - hi.astype(jnp.float32)).astype(jnp.bfloat16)
                z_hi[k1, pl.ds(r0, ROWS), i * LANES : (i + 1) * LANES] = hi
                z_lo[k1, pl.ds(r0, ROWS), i * LANES : (i + 1) * LANES] = lo

    def second(k1, rows):
        dims = (((1,), (1,)), ((), ()))
        hi, lo = z_hi[k1], z_lo[k1]
        w_hi, w_lo = table_ref[0, :rows, :], table_ref[1, :rows, :]
        dot = functools.partial(
            lax.dot_general, dimension_numbers=dims, preferred_element_type=jnp.float32
        )
        o = dot(w_hi, hi) + dot(w_hi, lo) + dot(w_lo, hi)
        for c in range(2):
            spec[c, pl.ds(k1, RADIX, stride=RADIX), :] = o[c * RADIX : (c + 1) * RADIX]
            if rows > 2 * RADIX:
                spec[c, pl.ds(RADIX - k1, RADIX, stride=RADIX), :] = o[
                    (2 + c) * RADIX : (3 + c) * RADIX
                ]

    second(0, 2 * RADIX)
    second(HALF, 2 * RADIX)

    @pl.loop(1, HALF)
    def _(k1):
        second(k1, 4 * RADIX)

    @pl.loop(0, groups)
    def _(g):
        for c in range(2):
            start = g * group
            for ref in out_refs:
                size = ref.shape[2]
                ref[g, c] = spec[c, pl.ds(pl.multiple_of(start, size), size), :].astype(jnp.bfloat16)
                start = start + size


def spectrum_of(old, mid, new, taps, groups, pieces):
    inputs = new[0].shape[0]
    length = taps.shape[1]
    assert length == RADIX * LANES and inputs == LANES and taps.shape[0] == 3
    channels = length // 2
    size = channels // groups // pieces
    twist, table = dft_tables(length)

    def block(index):
        return pl.BlockSpec((inputs, length), lambda i: (0, index))

    def whole(array):
        return pl.BlockSpec(array.shape, lambda i: (0,) * array.ndim)

    out = jax.ShapeDtypeStruct((groups, 2, size, inputs), jnp.bfloat16)
    return pl.pallas_call(
        fft_kernel,
        grid=(1,),
        out_shape=[out] * pieces,
        in_specs=[block(old[1]), block(mid[1]), block(new[1]), whole(taps), whole(twist), whole(table)],
        out_specs=[whole(out)] * pieces,
        scratch_shapes=[
            pltpu.VMEM((HALF + 1, inputs, 2 * LANES), jnp.bfloat16),
            pltpu.VMEM((HALF + 1, inputs, 2 * LANES), jnp.bfloat16),
            pltpu.VMEM((2, channels, inputs), jnp.float32),
        ],
        compiler_params=pltpu.CompilerParams(vmem_limit_bytes=VMEM_BYTES),
        cost_estimate=pl.CostEstimate(
            flops=12_000_000_000, bytes_accessed=8_000_000, transcendentals=0
        ),
    )(old[0], mid[0], new[0], taps, jnp.asarray(twist), jnp.asarray(table))


def pair_kernel(scale, pair_ref, late_ref, early_ref, pick_ref, *rest):
    out_ref, turned_left, turned_right, gram = rest[-4:]
    depth, chunk, inputs = late_ref.shape
    rows = depth * chunk
    depth = 2 * depth
    pairs = pair_ref.shape[0]
    half = depth // 2
    for i, ref in enumerate((late_ref, early_ref)):
        data = ref[...].reshape(rows, inputs)
        for side, turned in enumerate((turned_left, turned_right)):
            turned[i * rows : (i + 1) * rows, :] = jnp.dot(
                data, pick_ref[side], preferred_element_type=jnp.float32
            )
    lane_group = lax.broadcasted_iota(jnp.int32, (8, LANES), 1) // BLOCK_SIZE
    masks = [lane_group == j for j in range(4)]
    firsts = [pl.multiple_of(pair_ref[p, 0] * BLOCK_SIZE, BLOCK_SIZE) for p in range(pairs)]
    shifts = [
        [lax.rem(j - pair_ref[p, 1] + 4, 4) * BLOCK_SIZE for j in range(4)] for p in range(pairs)
    ]
    dims = (((0,), (0,)), ((), ()))
    unroll = gram.shape[0]

    @pl.loop(0, chunk // unroll)
    def _(step):
        for i in range(unroll):
            ch = step * unroll + i

            def operand(ref):
                re = ref[pl.ds(ch, half, stride=2 * chunk), :]
                im = ref[pl.ds(chunk + ch, half, stride=2 * chunk), :]
                return re, im

            re, im = operand(turned_left)
            left = jnp.concatenate([re, im], 0).astype(jnp.bfloat16)
            re, im = operand(turned_right)
            re, im = re * scale, im * scale
            right = jnp.concatenate(
                [jnp.concatenate([re, im], 0), jnp.concatenate([-im, re], 0)], 1
            ).astype(jnp.bfloat16)
            gram[i] = lax.dot_general(left, right, dims, preferred_element_type=jnp.float32)
        for i in range(unroll):
            ch = step * unroll + i
            for c in range(2):
                for p in range(pairs):
                    tile = None
                    for j in range(4):
                        piece = gram[
                            i, pl.ds(firsts[p] + 8 * j, 8), c * LANES : (c + 1) * LANES
                        ]
                        piece = pltpu.roll(piece, shifts[p][j], 1)
                        tile = piece if tile is None else jnp.where(masks[j], piece, tile)
                    out_ref[c, ch, pl.ds(p, 8, stride=pairs), :] = tile


def visibilities_of(late, early, base, pick, pair_list, scale, channels, earlier):
    depth, size, inputs = early.shape
    pairs = pair_list.shape[0]
    chunk = min(32, size)
    first = base // chunk
    operands = [pair_list, late, early, pick]
    in_specs = [
        pl.BlockSpec((depth, chunk, inputs), lambda i, _: (0, first + i, 0)),
        pl.BlockSpec((depth, chunk, inputs), lambda i, _: (0, i, 0)),
        pl.BlockSpec((2, inputs, inputs), lambda i, _: (0, 0, 0)),
    ]
    aliases = {}
    if earlier is not None:
        aliases = {len(operands): 0}
        operands.append(earlier)
        in_specs.append(pl.BlockSpec(memory_space=pl.ANY))
    return pl.pallas_call(
        functools.partial(pair_kernel, scale),
        grid_spec=pltpu.PrefetchScalarGridSpec(
            num_scalar_prefetch=1,
            grid=(size // chunk,),
            in_specs=in_specs,
            out_specs=pl.BlockSpec(
                (2, chunk, 8 * pairs, LANES), lambda i, _: (0, first + i, 0, 0)
            ),
            scratch_shapes=[
                pltpu.VMEM((2 * depth * chunk, inputs), jnp.float32),
                pltpu.VMEM((2 * depth * chunk, inputs), jnp.float32),
                pltpu.VMEM((min(UNROLL, chunk), inputs, 2 * inputs), jnp.float32),
            ],
        ),
        out_shape=jax.ShapeDtypeStruct((2, channels, 8 * pairs, LANES), jnp.float32),
        input_output_aliases=aliases,
        compiler_params=pltpu.CompilerParams(
            vmem_limit_bytes=VMEM_BYTES, dimension_semantics=("arbitrary",)
        ),
        cost_estimate=pl.CostEstimate(
            flops=20_000_000_000 // (channels // size), bytes_accessed=20_000_000, transcendentals=0
        ),
    )(*operands)


def input_order(station_order):
    return (2 * station_order[:, None] + jnp.arange(2, dtype=jnp.int32)[None, :]).reshape(-1)


def shards(row_count, voltages, taps, station_order, pair_list):
    order = input_order(station_order)
    inputs = voltages.shape[0]
    left_order = jnp.swapaxes(order.reshape(-1, BLOCK_SIZE // 4, 4), 1, 2).reshape(-1)
    both = jnp.stack([left_order, order])
    pick = (jnp.arange(inputs, dtype=jnp.int32)[None, :, None] == both[:, None, :]).astype(jnp.bfloat16)
    length = taps.shape[1]
    assert voltages.shape[1] == 2 * length
    onward = [(i, i + 1) for i in range(row_count - 1)]
    past_two = lax.ppermute(voltages[:, length:], "row", onward)
    sent, past_two = lax.optimization_barrier((voltages[:, :length], past_two))
    past_one = lax.ppermute(sent, "row", onward)
    channels = length // 2 // row_count
    pieces = min(PIECES, channels // 16)

    def exchange(piece):
        moved = lax.all_to_all(piece, "row", split_axis=0, concat_axis=0, tiled=True)
        return moved.reshape(2 * row_count, piece.shape[2], inputs)

    (second,) = spectrum_of((past_two, 0), (voltages, 0), (voltages, 1), taps, row_count, 1)
    second, past_one = lax.optimization_barrier((second, past_one))
    late = exchange(second)
    firsts = spectrum_of((past_one, 0), (past_two, 0), (voltages, 0), taps, row_count, pieces)
    result = None
    for index, piece in enumerate(firsts):
        early = exchange(piece)
        base = index * early.shape[1]
        result = visibilities_of(
            late, early, base, pick, pair_list, 1.0 / (2 * row_count), channels, result
        )
    pairs = pair_list.shape[0]
    tiles = result.reshape(2, channels, 8, pairs, LANES)
    return jnp.swapaxes(tiles, 2, 3).reshape(2, channels, pairs, BLOCK_SIZE * BLOCK_SIZE)


def solution(mesh):
    placed = (P("grp", "row"), P(), P("grp"), P("grp", None))
    return jax.shard_map(
        functools.partial(shards, mesh.shape["row"]),
        mesh=mesh,
        in_specs=placed,
        out_specs=P(None, "row", "grp", None),
        check_vma=False,
    )
```
